256 devices in a mesh: pts: 128 (over x, z, y), rep: 2 (over core).
Axes of the slice: x: 4, y: 4, z: 8, core: 2. Of those that a mesh axis runs over, the one named last changes fastest.
Arguments:
- feats: bfloat16 [2, 98304, 256], P('rep', 'pts'), may hold values from -6 to 6
- cotangent: bfloat16 [2, 98304, 256], P('rep', 'pts'), may hold values from -6 to 6
- dest: int32 [2, 98304], P('rep', 'pts'), may hold values from 0 to 131071, as said below
- pads: int32 [2, 128], P('rep', 'pts'), may hold values from 0 to 512, as said below
- w_qkv: bfloat16 [256, 768], replicated, may hold values from -24 to 24
- w_out: bfloat16 [256, 256], replicated, may hold values from -0.375 to 0.375
Outputs:
- result: bfloat16 [2, 98304, 256], P('rep', 'pts')
- grad_feats: bfloat16 [2, 98304, 256], P('rep', 'pts')
- grad_qkv: float32 [256, 768], replicated
- grad_out: float32 [256, 256], replicated
The draws below stay inside these ranges and needn't reach their ends.
Inputs may be any that keep to these rules, and one draw needn't show every extreme that they name: `dest`: each row's slot lies among the 1024 slots of one index of pts; every used slot is named exactly once; at most 10 points go from one index of pts to any one other index of pts, and in every draw some pair of indices reaches exactly 10. `pads`: the used slots of each scan number 98304.
All inputs are finite; a program needn't handle non-finite values.
Results may differ from the reference program's by a relative error of at most 0.015.
The reference program's roundings to bfloat16 on the way count: a program that leaves them out, or rounds other values in their place, can miss the bound.
Values may be sent and summed in bfloat16 or wider, within the bound.
A program may use at most 320 MiB of HBM per device.

```python
import jax
import jax.numpy as jnp
from jax import lax

D = 256
HEADS = 16
PATCH = 1024
PPD = 1
PTS_DEV = 768
POINTS = 98304
PATCHES = 128
N_PTS = 128
N_REP = 2


def regroup_tables(key):
    peer = PTS_DEV // N_PTS
    third = peer // 3
    base = peer - third
    reach = base // 2
    slot_dev = PPD * PATCH

    def one_scan(scan_key):
        keys = jax.random.split(scan_key, 4)
        lift = jax.random.randint(keys[0], (N_PTS,), 0, reach + 1)
        lift = lift.at[0].set(reach).at[1].set(0).at[2].set(reach)
        across = base + lift - jnp.roll(lift, -1)
        tilt = jax.random.randint(keys[1], (N_PTS,), 0, third + 1)
        tilt = tilt.at[0].set(third).at[1].set(0).at[2].set(third)
        extra = third + tilt - jnp.roll(tilt, -1)
        source = jnp.arange(N_PTS)[:, None]
        target = jnp.arange(N_PTS)[None, :]
        counts = across[(target - source) % N_PTS] + extra[None, :]
        column = jnp.sum(counts, axis=0)
        upto = jnp.cumsum(counts, axis=1)
        begin = upto - counts
        rowid = jnp.arange(PTS_DEV)
        owner = jnp.sum((rowid[None, :, None] >= upto[:, None, :]).astype(jnp.int32), axis=2)
        within = rowid[None, :] - jnp.take_along_axis(begin, owner, axis=1)
        before = jnp.cumsum(counts, axis=0) - counts
        offset = jnp.take_along_axis(before, owner, axis=1) + within
        patch_of = jnp.arange(slot_dev) // PATCH
        inside = jnp.arange(slot_dev) % PATCH
        filled = column[:, None] * (patch_of[None, :] + 1) // PPD - column[:, None] * patch_of[None, :] // PPD
        usable = inside[None, :] < filled
        scores = jax.random.randint(keys[2], (N_PTS, slot_dev), 0, 32768) * slot_dev + jnp.arange(slot_dev)[None, :]
        scores = scores + jnp.where(usable, 0, 2 ** 30)
        order = jnp.argsort(scores, axis=1).astype(jnp.int32)
        position = order[owner, offset]
        slots = owner * slot_dev + position
        shuffles = jax.vmap(lambda k: jax.random.permutation(k, PTS_DEV))(jax.random.split(keys[3], N_PTS))
        slots = jnp.take_along_axis(slots, shuffles, axis=1)
        patch_ids = jnp.arange(PPD)
        held = column[:, None] * (patch_ids[None, :] + 1) // PPD - column[:, None] * patch_ids[None, :] // PPD
        return (slots.reshape(-1).astype(jnp.int32), (PATCH - held).reshape(-1).astype(jnp.int32))
    return jax.vmap(one_scan)(jax.random.split(key, N_REP))


def draw_dest(key, part):
    tables = regroup_tables(key)
    return tables[0]


def draw_pads(key, part):
    tables = regroup_tables(key)
    return tables[1]


def draw_w_qkv(key, part):
    key = jax.random.fold_in(key, 7)
    weights = jnp.clip(jax.random.normal(key, (D, 3 * D), jnp.float32), -4.0, 4.0) * D ** (-0.5)
    return weights.astype(jnp.bfloat16)


def levels(own_key, extent, cuts, low, top_value):
    def one(dim, blocks):
        steps = jax.random.uniform(jax.random.fold_in(jax.random.fold_in(own_key, 6), dim), (blocks,), jnp.float32, low / len(cuts), top_value / len(cuts))
        return jnp.repeat(jnp.exp(steps), extent[dim] // blocks).reshape((-1,) + (1,) * (len(extent) - dim - 1))

    level = one(*cuts[0])
    for cut in cuts[1:]:
        level = level * one(*cut)
    return level


def noise(key, dims, scale, most, shards=(), kind=jnp.bfloat16):
    drawn = jax.random.normal(key, dims, jnp.float32) * scale
    if len(shards) > 0:
        drawn = levels(key, dims, shards, -0.22, 0.18) * drawn
    return jnp.clip(drawn, min=-most, max=most).astype(kind)


def setup_inputs(seed: int = 0) -> dict:
    streams_of = jax.random.split(jax.random.key(seed), 7)
    feats = noise(streams_of[0], (N_REP, POINTS, D), 1.0, 6.0, ((0, 2), (1, 128)))
    cotangent = noise(streams_of[1], (N_REP, POINTS, D), 1.0, 6.0, ((0, 2), (1, 128)))
    dest = draw_dest(jax.random.fold_in(streams_of[6], 71), 0)
    pads = draw_pads(jax.random.fold_in(streams_of[6], 71), 0)
    w_qkv = draw_w_qkv(jax.random.fold_in(streams_of[6], 71), 0)
    w_out = noise(streams_of[5], (D, D), D ** -0.5, 0.375)
    return {"feats": feats, "cotangent": cotangent, "dest": dest, "pads": pads, "w_qkv": w_qkv, "w_out": w_out}


def normalize(values):
    center = lax.optimization_barrier(jnp.mean(values, axis=-1, keepdims=True))
    spread = lax.optimization_barrier(jnp.mean(jnp.square(values - center), axis=-1, keepdims=True))
    return (values - center) * lax.rsqrt(spread + 1e-05)

def attend(qkv, keymask):
    count = qkv.shape[0]
    width = qkv.shape[1] // 3
    channels = width // HEADS
    parts = qkv.reshape(count, 3, HEADS, channels).transpose(1, 2, 0, 3)

    def one_head(item):
        query, keys, values = item
        scores = jnp.dot(query, keys.T, preferred_element_type=jnp.float32) * channels ** (-0.5)
        scores = jnp.where(keymask[None, :], scores, -1e+30)
        largest = lax.optimization_barrier(jnp.max(scores, axis=-1, keepdims=True))
        expo = jnp.exp(scores - largest)
        weights = (expo / lax.optimization_barrier(jnp.sum(expo, axis=-1, keepdims=True))).astype(jnp.bfloat16)
        return jnp.dot(weights, values, preferred_element_type=jnp.float32).astype(jnp.bfloat16)
    mixed = lax.map(one_head, (parts[0], parts[1], parts[2]))
    return mixed.transpose(1, 0, 2).reshape(count, width)

def forward(slot_rows, keymask, w_qkv, w_out):
    normed = normalize(slot_rows.astype(jnp.float32)).astype(jnp.bfloat16)
    qkv = jnp.dot(normed, w_qkv, preferred_element_type=jnp.float32).astype(jnp.bfloat16)
    attended = attend(qkv, keymask)
    out_rows = (slot_rows.astype(jnp.float32) + jnp.dot(attended, w_out, preferred_element_type=jnp.float32)).astype(jnp.bfloat16)
    return (out_rows, normed, qkv, attended)

def backward(cot_rows, slot_rows, normed, qkv, keymask, w_qkv, w_out):
    d_attended = jnp.dot(cot_rows, w_out.T, preferred_element_type=jnp.float32).astype(jnp.bfloat16)
    _, attend_back = jax.vjp(lambda packed: attend(packed, keymask), qkv)
    d_qkv = attend_back(d_attended)[0]
    grad_part = jnp.dot(normed.T, d_qkv, preferred_element_type=jnp.float32)
    d_normed = jnp.dot(d_qkv, w_qkv.T, preferred_element_type=jnp.float32)
    _, norm_back = jax.vjp(normalize, slot_rows.astype(jnp.float32))
    d_rows = (cot_rows.astype(jnp.float32) + norm_back(d_normed)[0]).astype(jnp.bfloat16)
    return (d_rows, grad_part)

def reference(feats, cotangent, dest, pads, w_qkv, w_out):
    total = N_PTS * PPD * PATCH
    scans = jnp.arange(N_REP)[:, None]

    def place(values):
        empty = jnp.zeros((N_REP, total, D), jnp.bfloat16)
        return empty.at[scans, dest].set(values).reshape(N_REP * PATCHES, PATCH, D)
    slot_feats = place(feats)
    slot_cot = place(cotangent)
    counts = (PATCH - pads).reshape(-1)
    masks = jnp.arange(PATCH)[None, :] < counts[:, None]

    def step(carry, item):
        slot_rows, cot_rows, keymask = item
        out_rows, normed, qkv, attended = forward(slot_rows, keymask, w_qkv, w_out)
        d_rows, grad_part = backward(cot_rows, slot_rows, normed, qkv, keymask, w_qkv, w_out)
        out_part = jnp.dot(attended.T, cot_rows, preferred_element_type=jnp.float32)
        return ((carry[0] + grad_part, carry[1] + out_part), (out_rows, d_rows))
    start = (jnp.zeros((D, 3 * D), jnp.float32), jnp.zeros((D, D), jnp.float32))
    sums, rows = lax.scan(step, start, (slot_feats, slot_cot, masks))
    out_all = rows[0].reshape(N_REP, total, D)
    grad_all = rows[1].reshape(N_REP, total, D)
    factor = (N_REP * POINTS) ** (-0.5)
    return (out_all[scans, dest], grad_all[scans, dest], sums[0] * factor, sums[1] * factor)
```

```python
import functools

import jax
import jax.numpy as jnp
from jax import lax
from jax.experimental import pallas as pl
from jax.experimental.pallas import tpu as pltpu
from jax.sharding import PartitionSpec as P

HEADS = 16
CH = 16
PATCH = 1024
CAP = 10
CHUNK = 24
BF = jnp.bfloat16
F32 = jnp.float32


def dg(a, b, ca, cb):
    return lax.dot_general(a, b, (((ca,), (cb,)), ((), ())), preferred_element_type=F32)


def iota(shape, dim):
    return lax.broadcasted_iota(jnp.int32, shape, dim)


def kernel(
    n, factor,
    feats, cot, dest, pads, w_qkv, w_out,
    out_r, out_g, out_wq, out_wo,
    pick, back, seat, stage, send_a, send_b, got_f, got_c, got_r, got_g,
    rows, x32, c16, norm, qkv, d_qkv, att, d_att, o32, inv, expo, d_s,
    grads, parts, total, other, whole,
    send_sem, recv_sem, pair_sem,
):
    me = lax.axis_index("pts")
    rep = lax.axis_index("rep")
    width = feats.shape[1]
    points = feats.shape[0]

    barrier = pltpu.get_barrier_semaphore()

    def greet(j, _):
        pl.semaphore_signal(
            barrier, inc=1, device_id=(lax.rem(me + j, n), rep), device_id_type=pl.DeviceIdType.MESH
        )
        return 0

    lax.fori_loop(1, n, greet, 0)
    pl.semaphore_signal(barrier, inc=1, device_id=(me, 1 - rep), device_id_type=pl.DeviceIdType.MESH)

    def chunk_copy(src, dst, which, peer):
        return pltpu.make_async_remote_copy(
            src_ref=src.at[peer],
            dst_ref=dst.at[me],
            send_sem=send_sem.at[which],
            recv_sem=recv_sem.at[which],
            device_id=(peer, rep),
            device_id_type=pl.DeviceIdType.MESH,
        )

    def send_some(src, dst, which, lo, hi):
        def one(j, _):
            chunk_copy(src, dst, which, lax.rem(me + j, n)).start()
            return 0

        lax.fori_loop(lo, hi, one, 0)

    def send_own(src, dst, which):
        pltpu.make_async_copy(src.at[me], dst.at[me], recv_sem.at[which]).start()

    def wait_got(dst, which):
        pltpu.make_async_copy(dst, dst, recv_sem.at[which]).wait()

    def wait_sent(src, which):
        part = src.at[pl.ds(0, n - 1)]
        pltpu.make_async_copy(part, part, send_sem.at[which]).wait()

    def to_chunks(values, dst):
        for k in range(CAP):
            for c in range(2):
                stage[pl.ds(c * CAP + k, n, stride=CHUNK), :] = values[
                    k * n : (k + 1) * n, c * 128 : (c + 1) * 128
                ]
        dst[...] = stage[...].reshape(n, CHUNK, 128).astype(BF)

    def from_chunks(src):
        stage[...] = src[...].astype(F32).reshape(n * CHUNK, 128)
        for k in range(CAP):
            for c in range(2):
                rows[k * n : (k + 1) * n, c * 128 : (c + 1) * 128] = stage[
                    pl.ds(c * CAP + k, n, stride=CHUNK), :
                ].astype(BF)

    target = dest[...]
    owner = lax.shift_right_logical(target, 10)
    code = (target & (PATCH - 1)) + 1
    owner_hot = (iota((n, points), 0) == owner).astype(F32).astype(BF)
    upper = (iota((points, points), 0) < iota((points, points), 1)).astype(F32).astype(BF)
    before = jnp.dot(owner_hot, upper, preferred_element_type=F32)
    rank = jnp.sum(before * owner_hot.astype(F32), axis=0, keepdims=True)
    place = rank * float(n) + owner.astype(F32)
    pick[...] = (iota((CAP * n, points), 0) == place.astype(jnp.int32)).astype(F32).astype(BF)
    high = lax.shift_right_logical(code, 5).astype(F32)
    low = (code & 31).astype(F32)
    lane = iota((128, points), 0).astype(F32)
    marks = (jnp.where(lane == rank, high, 0.0) + jnp.where(lane == rank + 16.0, low, 0.0)).astype(BF)
    stage[...] = jnp.zeros(stage.shape, F32)
    stage[pl.ds(2 * CAP, n, stride=CHUNK), :] = dg(owner_hot, marks, 1, 1)
    to_chunks(jnp.dot(pick[...], feats[...], preferred_element_type=F32), send_a)

    pl.semaphore_wait(barrier, n)

    send_some(send_a, got_f, 0, 1, n)
    send_own(send_a, got_f, 0)
    to_chunks(jnp.dot(pick[...], cot[...], preferred_element_type=F32), send_b)
    place_col = jnp.transpose(jnp.broadcast_to(place, (8, points)))[:, :1].astype(jnp.int32)
    back[...] = (iota((points, CAP * n), 1) == place_col).astype(F32).astype(BF)
    wait_got(got_f, 0)
    send_some(send_b, got_c, 1, 1, n)
    send_own(send_b, got_c, 1)

    from_chunks(got_f)
    marked = stage[pl.ds(2 * CAP, n, stride=CHUNK), :]
    for k in range(CAP):
        column = (32.0 * marked[:, k : k + 1] + marked[:, 16 + k : 17 + k]).astype(jnp.int32)
        seat[k * n : (k + 1) * n, :] = (iota((n, PATCH), 1) + 1 == column).astype(F32).astype(BF)
    x32[...] = dg(rows[...], seat[...], 0, 0)

    values = x32[...]
    center = jnp.mean(values, axis=0, keepdims=True)
    spread = jnp.mean(jnp.square(values - center), axis=0, keepdims=True)
    scale = lax.rsqrt(spread + 1e-05)
    norm[...] = ((values - center) * scale).astype(BF)
    qkv[...] = dg(w_qkv[...], norm[...], 0, 0).astype(BF)

    count = PATCH - pads[0, 0]
    first = iota((CH, PATCH), 0) == 0
    bias = jnp.where(first & (iota((CH, PATCH), 1) >= count), -1e30, 0.0).astype(BF)
    ones = jnp.where(iota((CH, PATCH), 0) == 0, 1.0, 0.0).astype(BF)
    pair = jnp.where(iota((CH, PATCH), 0) < 2, 1.0, 0.0).astype(BF)
    q_scale = float(CH ** -0.5 * 1.4426950408889634)
    half = PATCH // 2

    def forward(h, _):
        r = pl.multiple_of(h * CH, CH)
        q = qkv[pl.ds(r, CH), :].astype(F32) * q_scale
        k = qkv[pl.ds(width + r, CH), :]
        v = qkv[pl.ds(2 * width + r, CH), :]
        q_hi = q.astype(BF)
        q_lo = (q - q_hi.astype(F32)).astype(BF)
        left = jnp.concatenate([k, k, bias], axis=0)
        right = jnp.concatenate([q_hi, q_lo, ones], axis=0)
        for j in range(2):
            cols = slice(j * half, (j + 1) * half)
            s = dg(left, right[:, cols], 0, 0)
            m = jnp.max(s, axis=0, keepdims=True)
            e = jnp.exp2(s - m)
            reci = 1.0 / jnp.sum(e, axis=0, keepdims=True)
            e = e.astype(BF)
            expo[h, :, cols] = e
            inv[h, :, cols] = reci
            o32[pl.ds(r, CH), cols] = jnp.dot(v, e, preferred_element_type=F32) * reci
        return 0

    lax.fori_loop(0, HEADS, forward, 0)

    att[...] = o32[...].astype(BF)
    out_t = (x32[...] + dg(w_out[...], att[...], 0, 0)).astype(BF)
    wait_sent(send_a, 0)
    to_chunks(dg(seat[...], out_t, 1, 1), send_a)
    wait_got(got_c, 1)
    send_some(send_a, got_r, 2, 1, n)
    send_own(send_a, got_r, 2)
    from_chunks(got_c)
    c16[...] = dg(rows[...], seat[...], 0, 0).astype(BF)
    d_att[...] = jnp.dot(w_out[...], c16[...], preferred_element_type=F32).astype(BF)
    grads[:, 3 * width :] = dg(att[...], c16[...], 1, 1).astype(BF)

    def backward(h, _):
        r = pl.multiple_of(h * CH, CH)
        q = qkv[pl.ds(r, CH), :]
        k = qkv[pl.ds(width + r, CH), :]
        v = qkv[pl.ds(2 * width + r, CH), :]
        d_o = d_att[pl.ds(r, CH), :].astype(F32)
        reci = inv[h]
        delta = jnp.sum(d_o * o32[pl.ds(r, CH), :], axis=0, keepdims=True) * (-reci)
        d_o = d_o * reci
        d_hi = d_o.astype(BF)
        d_lo = (d_o - d_hi.astype(F32)).astype(BF)
        delta_hi = delta.astype(BF).astype(F32)
        delta_lo = delta - delta_hi
        row = iota((CH, PATCH), 0)
        extra = jnp.where(row == 0, delta_hi, jnp.where(row == 1, delta_lo, 0.0)).astype(BF)
        left = jnp.concatenate([v, v, pair], axis=0)
        right = jnp.concatenate([d_hi, d_lo, extra], axis=0)
        for j in range(2):
            cols = slice(j * half, (j + 1) * half)
            t = dg(left, right[:, cols], 0, 0)
            e = (expo[h, :, cols].astype(F32) * t).astype(BF)
            d_s[:, cols] = e
            d_qkv[pl.ds(r, CH), cols] = (jnp.dot(k, e, preferred_element_type=F32) * 0.25).astype(BF)
        d_qkv[pl.ds(2 * width + r, CH), :] = dg(d_hi, expo[h], 1, 1).astype(BF)
        d_qkv[pl.ds(width + r, CH), :] = (dg(q, d_s[...], 1, 1) * 0.25).astype(BF)
        return 0

    lax.fori_loop(0, HEADS, backward, 0)

    grads[:, : 3 * width] = dg(norm[...], d_qkv[...], 1, 1).astype(BF)

    def block(ref, p):
        return ref.at[
            pl.ds(pl.multiple_of((p // 8) * 16, 16), 16), pl.ds(pl.multiple_of((p % 8) * 128, 128), 128)
        ]

    def spread_part(j, _):
        peer = lax.rem(me + j, n)
        pltpu.make_async_remote_copy(
            src_ref=block(grads, peer),
            dst_ref=parts.at[me],
            send_sem=send_sem.at[4],
            recv_sem=recv_sem.at[4],
            device_id=(peer, rep),
            device_id_type=pl.DeviceIdType.MESH,
        ).start()
        return 0

    lax.fori_loop(1, n, spread_part, 0)
    pltpu.make_async_copy(block(grads, me), parts.at[me], recv_sem.at[4]).start()

    d_norm = jnp.dot(w_qkv[...], d_qkv[...], preferred_element_type=F32)
    values = x32[...]
    center = jnp.mean(values, axis=0, keepdims=True)
    spread = jnp.mean(jnp.square(values - center), axis=0, keepdims=True)
    scale = lax.rsqrt(spread + 1e-05)
    unit = (values - center) * scale
    along = jnp.mean(d_norm * unit, axis=0, keepdims=True)
    level = jnp.mean(d_norm, axis=0, keepdims=True)
    d_rows = (c16[...].astype(F32) + scale * (d_norm - level - unit * along)).astype(BF)
    wait_sent(send_b, 1)
    to_chunks(dg(seat[...], d_rows, 1, 1), send_b)
    send_some(send_b, got_g, 3, 1, n)
    send_own(send_b, got_g, 3)

    wait_got(parts, 4)
    total[...] = jnp.sum(parts[...].astype(F32), axis=0)
    swap = pltpu.make_async_remote_copy(
        src_ref=total, dst_ref=other, send_sem=pair_sem.at[0], recv_sem=pair_sem.at[1],
        device_id=(me, 1 - rep), device_id_type=pl.DeviceIdType.MESH,
    )
    swap.start()
    swap.wait()
    mine = ((total[...] + other[...]) * factor).astype(BF)
    parts[0] = mine

    def share(j, _):
        peer = lax.rem(me + j, n)
        pltpu.make_async_remote_copy(
            src_ref=parts.at[0],
            dst_ref=block(whole, me),
            send_sem=send_sem.at[5],
            recv_sem=recv_sem.at[5],
            device_id=(peer, rep),
            device_id_type=pl.DeviceIdType.MESH,
        ).start()
        return 0

    lax.fori_loop(1, n, share, 0)
    pltpu.make_async_copy(parts.at[0], block(whole, me), recv_sem.at[5]).start()

    wait_got(got_r, 2)
    from_chunks(got_r)
    out_r[...] = jnp.dot(back[...], rows[...], preferred_element_type=F32).astype(BF)
    wait_got(got_g, 3)
    from_chunks(got_g)
    out_g[...] = jnp.dot(back[...], rows[...], preferred_element_type=F32).astype(BF)
    pltpu.make_async_copy(whole, whole, recv_sem.at[5]).wait()
    out_wq[...] = whole[:, : 3 * width].astype(F32)
    out_wo[...] = whole[:, 3 * width :].astype(F32)
    wait_sent(send_a, 2)
    wait_sent(send_b, 3)
    wait_sent(parts, 4)
    wait_sent(parts, 5)


def on_device(feats, cotangent, dest, pads, w_qkv, w_out):
    n = lax.axis_size("pts")
    points = feats.shape[1]
    width = feats.shape[2]
    factor = float((n * lax.axis_size("rep") * points) ** (-0.5))
    vmem = pl.BlockSpec(memory_space=pltpu.VMEM)
    got = pl.pallas_call(
        functools.partial(kernel, n, factor),
        out_shape=(
            jax.ShapeDtypeStruct((points, width), BF),
            jax.ShapeDtypeStruct((points, width), BF),
            jax.ShapeDtypeStruct((width, 3 * width), F32),
            jax.ShapeDtypeStruct((width, width), F32),
        ),
        in_specs=[vmem, vmem, vmem, pl.BlockSpec(memory_space=pltpu.SMEM), vmem, vmem],
        out_specs=(vmem, vmem, vmem, vmem),
        scratch_shapes=[
            pltpu.VMEM((CAP * n, points), BF),
            pltpu.VMEM((points, CAP * n), BF),
            pltpu.VMEM((CAP * n, PATCH), BF),
            pltpu.VMEM((n * CHUNK, 128), F32),
            *[pltpu.VMEM((n, CHUNK, 128), BF)] * 6,
            pltpu.VMEM((CAP * n, width), BF),
            pltpu.VMEM((width, PATCH), F32),
            pltpu.VMEM((width, PATCH), BF),
            pltpu.VMEM((width, PATCH), BF),
            pltpu.VMEM((3 * width, PATCH), BF),
            pltpu.VMEM((3 * width, PATCH), BF),
            pltpu.VMEM((width, PATCH), BF),
            pltpu.VMEM((width, PATCH), BF),
            pltpu.VMEM((width, PATCH), F32),
            pltpu.VMEM((HEADS, 1, PATCH), F32),
            pltpu.VMEM((HEADS, PATCH, PATCH), BF),
            pltpu.VMEM((PATCH, PATCH), BF),
            pltpu.VMEM((width, 4 * width), BF),
            pltpu.VMEM((n, 16, 128), BF),
            pltpu.VMEM((16, 128), F32),
            pltpu.VMEM((16, 128), F32),
            pltpu.VMEM((width, 4 * width), BF),
            pltpu.SemaphoreType.DMA((6,)),
            pltpu.SemaphoreType.DMA((6,)),
            pltpu.SemaphoreType.DMA((2,)),
        ],
        compiler_params=pltpu.CompilerParams(
            collective_id=0, has_side_effects=True, vmem_limit_bytes=62 * 2**20
        ),
        cost_estimate=pl.CostEstimate(flops=4 * 10**9, bytes_accessed=4 * 10**6, transcendentals=17 * 10**6),
    )(feats[0], cotangent[0], dest, pads, w_qkv, w_out)
    return (got[0][None], got[1][None], got[2], got[3])


def solution(mesh):
    placed = (
        P("rep", "pts", None),
        P("rep", "pts", None),
        P("rep", "pts"),
        P("rep", "pts"),
        P(),
        P(),
    )
    return jax.shard_map(
        on_device,
        mesh=mesh,
        in_specs=placed,
        out_specs=(P("rep", "pts", None), P("rep", "pts", None), P(), P()),
        check_vma=False,
    )
```

```python
import functools

import jax
import jax.numpy as jnp
from jax import lax
from jax.experimental import pallas as pl
from jax.experimental.pallas import tpu as pltpu
from jax.sharding import PartitionSpec as P

HEADS = 16
CH = 16
PATCH = 1024
CAP = 10
CHUNK = 24
EARLY = 10
MIX = 45
UNMIX = 37
BF = jnp.bfloat16
F32 = jnp.float32


def dg(a, b, ca, cb):
    return lax.dot_general(a, b, (((ca,), (cb,)), ((), ())), preferred_element_type=F32)


def iota(shape, dim):
    return lax.broadcasted_iota(jnp.int32, shape, dim)


def kernel(
    n, factor,
    feats, cot, dest, pads, w_qkv, w_out,
    out_r, out_g, out_wq, out_wo,
    back, seat, stage, send_a, send_b, got_f, got_c, got_r, got_g,
    rows, x16, c16, norm, qkv, att, d_att, o32, inv, expo,
    grads, parts, total, other, whole,
    send_sem, recv_sem, pair_sem,
):
    me = lax.axis_index("pts")
    rep = lax.axis_index("rep")
    width = feats.shape[1]
    points = feats.shape[0]

    barrier = pltpu.get_barrier_semaphore()

    def greet(j, _):
        pl.semaphore_signal(
            barrier, inc=1, device_id=(lax.rem(me + j, n), rep), device_id_type=pl.DeviceIdType.MESH
        )
        return 0

    lax.fori_loop(1, n, greet, 0)
    pl.semaphore_signal(barrier, inc=1, device_id=(me, 1 - rep), device_id_type=pl.DeviceIdType.MESH)

    def chunk_copy(src, dst, which, peer):
        return pltpu.make_async_remote_copy(
            src_ref=src.at[peer],
            dst_ref=dst.at[me],
            send_sem=send_sem.at[which],
            recv_sem=recv_sem.at[which],
            device_id=(peer, rep),
            device_id_type=pl.DeviceIdType.MESH,
        )

    def send_some(src, dst, which, lo, hi):
        def one(j, _):
            chunk_copy(src, dst, which, lax.rem(me + j, n)).start()
            return 0

        lax.fori_loop(lo, hi, one, 0)

    def send_own(src, dst, which):
        pltpu.make_async_copy(src.at[me], dst.at[me], recv_sem.at[which]).start()

    def wait_got(dst, which):
        pltpu.make_async_copy(dst, dst, recv_sem.at[which]).wait()

    def wait_sent(src, which):
        part = src.at[pl.ds(0, n - 1)]
        pltpu.make_async_copy(part, part, send_sem.at[which]).wait()

    def to_chunks(values, dst):
        for k in range(CAP):
            for c in range(2):
                stage[pl.ds(c * CAP + k, n, stride=CHUNK), :] = values[
                    k * n : (k + 1) * n, c * 128 : (c + 1) * 128
                ]
        dst[...] = stage[...].reshape(n, CHUNK, 128).astype(BF)

    def from_chunks(src):
        stage[...] = src[...].astype(F32).reshape(n * CHUNK, 128)
        for k in range(CAP):
            for c in range(2):
                rows[k * n : (k + 1) * n, c * 128 : (c + 1) * 128] = stage[
                    pl.ds(c * CAP + k, n, stride=CHUNK), :
                ].astype(BF)

    target = dest[...]
    owner = lax.shift_right_logical(target, 10)
    code = (target & (PATCH - 1)) + 1
    owner_hot = (iota((n, points), 0) == owner).astype(F32).astype(BF)
    upper = (iota((points, points), 0) < iota((points, points), 1)).astype(F32).astype(BF)
    before = jnp.dot(owner_hot, upper, preferred_element_type=F32)
    rank = jnp.sum(before * owner_hot.astype(F32), axis=0, keepdims=True)
    place = rank * float(n) + owner.astype(F32)
    pick = (iota((CAP * n, points), 0) == place.astype(jnp.int32)).astype(F32).astype(BF)
    high = lax.shift_right_logical(code, 5).astype(F32)
    low = (code & 31).astype(F32)
    lane = iota((128, points), 0).astype(F32)
    marks = (jnp.where(lane == rank, high, 0.0) + jnp.where(lane == rank + 16.0, low, 0.0)).astype(BF)
    stage[...] = jnp.zeros(stage.shape, F32)
    stage[pl.ds(2 * CAP, n, stride=CHUNK), :] = dg(owner_hot, marks, 1, 1)
    to_chunks(jnp.dot(pick, feats[...], preferred_element_type=F32), send_a)
    to_chunks(jnp.dot(pick, cot[...], preferred_element_type=F32), send_b)

    pl.semaphore_wait(barrier, n)

    send_some(send_a, got_f, 0, 1, n)
    send_own(send_a, got_f, 0)
    place_col = jnp.transpose(jnp.broadcast_to(place, (8, points)))[:, :1].astype(jnp.int32)
    back[...] = (iota((points, CAP * n), 1) == place_col).astype(F32).astype(BF)
    wait_got(got_f, 0)
    send_some(send_b, got_c, 1, 1, 2)
    send_own(send_b, got_c, 1)

    from_chunks(got_f)
    marked = stage[pl.ds(2 * CAP, n, stride=CHUNK), :]
    for k in range(CAP):
        column = (32.0 * marked[:, k : k + 1] + marked[:, 16 + k : 17 + k]).astype(jnp.int32)
        seat[k * n : (k + 1) * n, :] = (iota((n, PATCH), 1) + 1 == column).astype(F32).astype(BF)
    x16[...] = dg(rows[...], seat[...], 0, 0).astype(BF)

    values = x16[...].astype(F32)
    center = jnp.mean(values, axis=0, keepdims=True)
    spread = jnp.mean(jnp.square(values - center), axis=0, keepdims=True)
    scale = lax.rsqrt(spread + 1e-05)
    norm[...] = ((values - center) * scale).astype(BF)
    qkv[...] = dg(w_qkv[...], norm[...], 0, 0).astype(BF)

    count = PATCH - pads[0, 0]
    first = iota((CH, PATCH), 0) == 0
    bias = jnp.where(first & (iota((CH, PATCH), 1) >= count), -1e30, 0.0).astype(BF)
    ones = jnp.where(iota((CH, PATCH), 0) == 0, 1.0, 0.0).astype(BF)
    pair = jnp.where(iota((CH, PATCH), 0) < 2, 1.0, 0.0).astype(BF)
    q_scale = float(CH ** -0.5 * 1.4426950408889634)

    def forward(step, first_peer, sends):
        for i in range(sends):
            chunk_copy(send_b, got_c, 1, lax.rem(me + first_peer + step * sends + i, n)).start()
        pending = None
        for u in range(2):
            h = step * 2 + u
            r = pl.multiple_of(h * CH, CH)
            q = qkv[pl.ds(r, CH), :].astype(F32) * q_scale
            k = qkv[pl.ds(width + r, CH), :]
            v = qkv[pl.ds(2 * width + r, CH), :]
            q_hi = q.astype(BF)
            q_lo = (q - q_hi.astype(F32)).astype(BF)
            left = jnp.concatenate([k, k, bias], axis=0)
            right = jnp.concatenate([q_hi, q_lo, ones], axis=0)
            s = dg(left, right, 0, 0)
            if pending is not None:
                pending()
            m = jnp.max(s, axis=0, keepdims=True)
            e = jnp.exp2(s - m)
            reci = 1.0 / jnp.sum(e, axis=0, keepdims=True)
            e = e.astype(BF)
            expo[h] = e
            inv[h] = reci

            def pending(r=r, v=v, e=e, reci=reci):
                o32[pl.ds(r, CH), :] = jnp.dot(v, e, preferred_element_type=F32) * reci

        pending()

    def forward_sending(step, _):
        forward(step, 2, 21)
        return 0

    def forward_plain(step, _):
        forward(step, 0, 0)
        return 0

    lax.fori_loop(0, 6, forward_sending, 0)
    lax.fori_loop(6, HEADS // 2, forward_plain, 0)

    att[...] = o32[...].astype(BF)
    out_t = (x16[...].astype(F32) + dg(w_out[...], att[...], 0, 0)).astype(BF)
    wait_sent(send_a, 0)
    to_chunks(dg(seat[...], out_t, 1, 1), send_a)
    wait_got(got_c, 1)
    send_some(send_a, got_r, 2, 1, 3)
    send_own(send_a, got_r, 2)
    from_chunks(got_c)
    c16[...] = dg(rows[...], seat[...], 0, 0).astype(BF)
    d_att[...] = jnp.dot(w_out[...], c16[...], preferred_element_type=F32).astype(BF)
    grads[:width, :] = dg(att[...], c16[...], 1, 1).astype(BF)

    def backward(step, first_peer, sends):
        for i in range(sends):
            chunk_copy(send_a, got_r, 2, lax.rem(me + first_peer + step * sends + i, n)).start()
        row = iota((CH, PATCH), 0)
        pending = None
        for u in range(2):
            h = step * 2 + u
            r = pl.multiple_of(h * CH, CH)
            q = qkv[pl.ds(r, CH), :]
            k = qkv[pl.ds(width + r, CH), :]
            v = qkv[pl.ds(2 * width + r, CH), :]
            d_o = d_att[pl.ds(r, CH), :].astype(F32)
            reci = inv[h]
            delta = jnp.sum(d_o * o32[pl.ds(r, CH), :], axis=0, keepdims=True) * (-reci)
            d_o = d_o * reci
            d_hi = d_o.astype(BF)
            d_lo = (d_o - d_hi.astype(F32)).astype(BF)
            delta_hi = delta.astype(BF).astype(F32)
            delta_lo = delta - delta_hi
            extra = jnp.where(row == 0, delta_hi, jnp.where(row == 1, delta_lo, 0.0)).astype(BF)
            left = jnp.concatenate([v, v, pair], axis=0)
            right = jnp.concatenate([d_hi, d_lo, extra], axis=0)
            t = dg(left, right, 0, 0)
            d_v = dg(d_hi, expo[h], 1, 1)
            e = (expo[h].astype(F32) * t).astype(BF)
            if pending is not None:
                pending()
            expo[h] = e
            qkv[pl.ds(2 * width + r, CH), :] = d_v.astype(BF)

            def pending(r=r, k=k, q=q, h=h):
                e = expo[h]
                qkv[pl.ds(r, CH), :] = (jnp.dot(k, e, preferred_element_type=F32) * 0.25).astype(BF)
                qkv[pl.ds(width + r, CH), :] = (dg(q, e, 1, 1) * 0.25).astype(BF)

        pending()

    def backward_sending(step, _):
        backward(step, 3, 25)
        return 0

    def backward_plain(step, _):
        backward(step, 0, 0)
        return 0

    early = EARLY * CH
    late = width - early
    tiles = (width + 3 * early) // 8
    mine = lax.rem(me * UNMIX, n)
    is_early = mine < tiles

    def tile(ref, t):
        return ref.at[
            pl.ds(pl.multiple_of((t // 2) * 16, 16), 16), pl.ds(pl.multiple_of((t % 2) * 128, 128), 128)
        ]

    def send_tiles(lo, hi):
        def one(j, _):
            t = lo + lax.rem(j + me, hi - lo)
            peer = lax.rem(t * MIX, n)

            @pl.when(peer != me)
            def _():
                pltpu.make_async_remote_copy(
                    src_ref=tile(grads, t),
                    dst_ref=parts.at[me],
                    send_sem=send_sem.at[4],
                    recv_sem=recv_sem.at[4],
                    device_id=(peer, rep),
                    device_id_type=pl.DeviceIdType.MESH,
                ).start()

            @pl.when(peer == me)
            def _():
                pltpu.make_async_copy(tile(grads, mine), parts.at[me], recv_sem.at[4]).start()

            return 0

        lax.fori_loop(0, hi - lo, one, 0)

    def swap():
        return pltpu.make_async_remote_copy(
            src_ref=total, dst_ref=other, send_sem=pair_sem.at[0], recv_sem=pair_sem.at[1],
            device_id=(me, 1 - rep), device_id_type=pl.DeviceIdType.MESH,
        )

    def sum_tile():
        wait_got(parts, 4)
        total[...] = jnp.sum(parts[...].astype(F32), axis=0)
        swap().start()

    def share_tile():
        swap().wait()
        parts[0] = ((total[...] + other[...]) * factor).astype(BF)

        def one(j, _):
            pltpu.make_async_remote_copy(
                src_ref=parts.at[0],
                dst_ref=tile(whole, mine),
                send_sem=send_sem.at[5],
                recv_sem=recv_sem.at[5],
                device_id=(lax.rem(me + j, n), rep),
                device_id_type=pl.DeviceIdType.MESH,
            ).start()
            return 0

        lax.fori_loop(1, n, one, 0)
        pltpu.make_async_copy(parts.at[0], tile(whole, mine), recv_sem.at[5]).start()

    lax.fori_loop(0, EARLY // 2, backward_sending, 0)
    at = width
    for p in range(3):
        grads[at : at + early, :] = dg(
            qkv[p * width : p * width + early, :], norm[...], 1, 1
        ).astype(BF)
        at += early
    send_tiles(0, tiles)
    backward_plain(EARLY // 2, 0)
    pl.when(is_early)(sum_tile)
    backward_plain(EARLY // 2 + 1, 0)
    pl.when(is_early)(share_tile)
    lax.fori_loop(EARLY // 2 + 2, HEADS // 2, backward_plain, 0)
    for p in range(3):
        grads[at : at + late, :] = dg(
            qkv[p * width + early : (p + 1) * width, :], norm[...], 1, 1
        ).astype(BF)
        at += late
    send_tiles(tiles, n)

    d_norm = jnp.dot(w_qkv[...], qkv[...], preferred_element_type=F32)
    values = x16[...].astype(F32)
    center = jnp.mean(values, axis=0, keepdims=True)
    spread = jnp.mean(jnp.square(values - center), axis=0, keepdims=True)
    scale = lax.rsqrt(spread + 1e-05)
    unit = (values - center) * scale
    along = jnp.mean(d_norm * unit, axis=0, keepdims=True)
    level = jnp.mean(d_norm, axis=0, keepdims=True)
    d_rows = (c16[...].astype(F32) + scale * (d_norm - level - unit * along)).astype(BF)
    wait_sent(send_b, 1)
    to_chunks(dg(seat[...], d_rows, 1, 1), send_b)
    send_some(send_b, got_g, 3, 1, n)
    send_own(send_b, got_g, 3)

    pl.when(jnp.logical_not(is_early))(sum_tile)
    wait_got(got_r, 2)
    from_chunks(got_r)
    out_r[...] = jnp.dot(back[...], rows[...], preferred_element_type=F32).astype(BF)
    pl.when(jnp.logical_not(is_early))(share_tile)
    wait_got(got_g, 3)
    from_chunks(got_g)
    out_g[...] = jnp.dot(back[...], rows[...], preferred_element_type=F32).astype(BF)
    pltpu.make_async_copy(whole, whole, recv_sem.at[5]).wait()
    pieces = []
    for p in range(3):
        at = width + p * early
        pieces.append(whole[at : at + early, :])
        at = width + 3 * early + p * late
        pieces.append(whole[at : at + late, :])
    out_wq[...] = jnp.transpose(jnp.concatenate(pieces, axis=0).astype(F32))
    out_wo[...] = whole[:width, :].astype(F32)
    wait_sent(send_a, 2)
    wait_sent(send_b, 3)
    wait_sent(parts, 4)
    wait_sent(parts, 5)


def on_device(feats, cotangent, dest, pads, w_qkv, w_out):
    n = lax.axis_size("pts")
    points = feats.shape[1]
    width = feats.shape[2]
    factor = float((n * lax.axis_size("rep") * points) ** (-0.5))
    vmem = pl.BlockSpec(memory_space=pltpu.VMEM)
    got = pl.pallas_call(
        functools.partial(kernel, n, factor),
        out_shape=(
            jax.ShapeDtypeStruct((points, width), BF),
            jax.ShapeDtypeStruct((points, width), BF),
            jax.ShapeDtypeStruct((width, 3 * width), F32),
            jax.ShapeDtypeStruct((width, width), F32),
        ),
        in_specs=[vmem, vmem, vmem, pl.BlockSpec(memory_space=pltpu.SMEM), vmem, vmem],
        out_specs=(vmem, vmem, vmem, vmem),
        scratch_shapes=[
            pltpu.VMEM((points, CAP * n), BF),
            pltpu.VMEM((CAP * n, PATCH), BF),
            pltpu.VMEM((n * CHUNK, 128), F32),
            *[pltpu.VMEM((n, CHUNK, 128), BF)] * 6,
            pltpu.VMEM((CAP * n, width), BF),
            pltpu.VMEM((width, PATCH), BF),
            pltpu.VMEM((width, PATCH), BF),
            pltpu.VMEM((width, PATCH), BF),
            pltpu.VMEM((3 * width, PATCH), BF),
            pltpu.VMEM((width, PATCH), BF),
            pltpu.VMEM((width, PATCH), BF),
            pltpu.VMEM((width, PATCH), F32),
            pltpu.VMEM((HEADS, 1, PATCH), F32),
            pltpu.VMEM((HEADS, PATCH, PATCH), BF),
            pltpu.VMEM((4 * width, width), BF),
            pltpu.VMEM((n, 16, 128), BF),
            pltpu.VMEM((16, 128), F32),
            pltpu.VMEM((16, 128), F32),
            pltpu.VMEM((4 * width, width), BF),
            pltpu.SemaphoreType.DMA((6,)),
            pltpu.SemaphoreType.DMA((6,)),
            pltpu.SemaphoreType.DMA((2,)),
        ],
        compiler_params=pltpu.CompilerParams(
            collective_id=0, has_side_effects=True, vmem_limit_bytes=62 * 2**20
        ),
        cost_estimate=pl.CostEstimate(flops=4 * 10**9, bytes_accessed=4 * 10**6, transcendentals=17 * 10**6),
    )(feats[0], cotangent[0], dest, pads, w_qkv, w_out)
    return (got[0][None], got[1][None], got[2], got[3])


def solution(mesh):
    placed = (
        P("rep", "pts", None),
        P("rep", "pts", None),
        P("rep", "pts"),
        P("rep", "pts"),
        P(),
        P(),
    )
    return jax.shard_map(
        on_device,
        mesh=mesh,
        in_specs=placed,
        out_specs=(P("rep", "pts", None), P("rep", "pts", None), P(), P()),
        check_vma=False,
    )
```

```python
import functools

import jax
import jax.numpy as jnp
from jax import lax
from jax.experimental import pallas as pl
from jax.experimental.pallas import tpu as pltpu
from jax.sharding import PartitionSpec as P

HEADS = 16
CH = 16
PATCH = 1024
CAP = 10
CHUNK = 24
EARLY = 8
RING = 8
SIDE = 4
PLANE = SIDE * SIDE
MIX = 7
BF = jnp.bfloat16
F32 = jnp.float32


def dg(a, b, ca, cb):
    return lax.dot_general(a, b, (((ca,), (cb,)), ((), ())), preferred_element_type=F32)


def iota(shape, dim):
    return lax.broadcasted_iota(jnp.int32, shape, dim)


def kernel(
    n, factor,
    feats, cot, dest, pads, w_qkv, w_out,
    out_r, out_g, out_wq, out_wo,
    back, seat, stage, send_a, send_b, got_f, got_c, got_r, got_g,
    rows, x16, c16, norm, qkv, att, d_att, o32, inv, expo,
    grads, parts, plane_sum, strips, total, other, scaled, done, ready, whole,
    send_sem, recv_sem, pair_sem,
):
    me = lax.axis_index("pts")
    rep = lax.axis_index("rep")
    width = feats.shape[1]
    points = feats.shape[0]

    barrier = pltpu.get_barrier_semaphore()

    def greet(j, _):
        pl.semaphore_signal(
            barrier, inc=1, device_id=(lax.rem(me + j, n), rep), device_id_type=pl.DeviceIdType.MESH
        )
        return 0

    lax.fori_loop(1, n, greet, 0)
    pl.semaphore_signal(barrier, inc=1, device_id=(me, 1 - rep), device_id_type=pl.DeviceIdType.MESH)

    def chunk_copy(src, dst, which, peer):
        return pltpu.make_async_remote_copy(
            src_ref=src.at[peer],
            dst_ref=dst.at[me],
            send_sem=send_sem.at[which],
            recv_sem=recv_sem.at[which],
            device_id=(peer, rep),
            device_id_type=pl.DeviceIdType.MESH,
        )

    def send_some(src, dst, which, lo, hi):
        def one(j, _):
            chunk_copy(src, dst, which, lax.rem(me + j, n)).start()
            return 0

        lax.fori_loop(lo, hi, one, 0)

    def send_own(src, dst, which):
        pltpu.make_async_copy(src.at[me], dst.at[me], recv_sem.at[which]).start()

    def wait_got(dst, which):
        pltpu.make_async_copy(dst, dst, recv_sem.at[which]).wait()

    def wait_sent(src, which):
        part = src.at[pl.ds(0, n - 1)]
        pltpu.make_async_copy(part, part, send_sem.at[which]).wait()

    def to_chunks(values, dst):
        for k in range(CAP):
            for c in range(2):
                stage[pl.ds(c * CAP + k, n, stride=CHUNK), :] = values[
                    k * n : (k + 1) * n, c * 128 : (c + 1) * 128
                ]
        dst[...] = stage[...].reshape(n, CHUNK, 128).astype(BF)

    def from_chunks(src):
        stage[...] = src[...].astype(F32).reshape(n * CHUNK, 128)
        for k in range(CAP):
            for c in range(2):
                rows[k * n : (k + 1) * n, c * 128 : (c + 1) * 128] = stage[
                    pl.ds(c * CAP + k, n, stride=CHUNK), :
                ].astype(BF)

    target = dest[...]
    owner = lax.shift_right_logical(target, 10)
    code = (target & (PATCH - 1)) + 1
    owner_hot = (iota((n, points), 0) == owner).astype(F32).astype(BF)
    upper = (iota((points, points), 0) < iota((points, points), 1)).astype(F32).astype(BF)
    before = jnp.dot(owner_hot, upper, preferred_element_type=F32)
    rank = jnp.sum(before * owner_hot.astype(F32), axis=0, keepdims=True)
    place = rank * float(n) + owner.astype(F32)
    pick = (iota((CAP * n, points), 0) == place.astype(jnp.int32)).astype(F32).astype(BF)
    high = lax.shift_right_logical(code, 5).astype(F32)
    low = (code & 31).astype(F32)
    lane = iota((128, points), 0).astype(F32)
    marks = (jnp.where(lane == rank, high, 0.0) + jnp.where(lane == rank + 16.0, low, 0.0)).astype(BF)
    stage[...] = jnp.zeros(stage.shape, F32)
    stage[pl.ds(2 * CAP, n, stride=CHUNK), :] = dg(owner_hot, marks, 1, 1)
    to_chunks(jnp.dot(pick, feats[...], preferred_element_type=F32), send_a)
    to_chunks(jnp.dot(pick, cot[...], preferred_element_type=F32), send_b)

    pl.semaphore_wait(barrier, n)

    send_some(send_a, got_f, 0, 1, n)
    send_own(send_a, got_f, 0)
    place_col = jnp.transpose(jnp.broadcast_to(place, (8, points)))[:, :1].astype(jnp.int32)
    back[...] = (iota((points, CAP * n), 1) == place_col).astype(F32).astype(BF)
    wait_got(got_f, 0)
    send_some(send_b, got_c, 1, 1, 2)
    send_own(send_b, got_c, 1)

    from_chunks(got_f)
    marked = stage[pl.ds(2 * CAP, n, stride=CHUNK), :]
    for k in range(CAP):
        column = (32.0 * marked[:, k : k + 1] + marked[:, 16 + k : 17 + k]).astype(jnp.int32)
        seat[k * n : (k + 1) * n, :] = (iota((n, PATCH), 1) + 1 == column).astype(F32).astype(BF)
    x16[...] = dg(rows[...], seat[...], 0, 0).astype(BF)

    values = x16[...].astype(F32)
    center = jnp.mean(values, axis=0, keepdims=True)
    spread = jnp.mean(jnp.square(values - center), axis=0, keepdims=True)
    scale = lax.rsqrt(spread + 1e-05)
    norm[...] = ((values - center) * scale).astype(BF)
    qkv[...] = dg(w_qkv[...], norm[...], 0, 0).astype(BF)

    count = PATCH - pads[0, 0]
    first = iota((CH, PATCH), 0) == 0
    bias = jnp.where(first & (iota((CH, PATCH), 1) >= count), -1e30, 0.0).astype(BF)
    ones = jnp.where(iota((CH, PATCH), 0) == 0, 1.0, 0.0).astype(BF)
    pair = jnp.where(iota((CH, PATCH), 0) < 2, 1.0, 0.0).astype(BF)
    q_scale = float(CH ** -0.5 * 1.4426950408889634)

    def forward(step, first_peer, sends):
        for i in range(sends):
            chunk_copy(send_b, got_c, 1, lax.rem(me + first_peer + step * sends + i, n)).start()
        pending = None
        for u in range(2):
            h = step * 2 + u
            r = pl.multiple_of(h * CH, CH)
            q = qkv[pl.ds(r, CH), :].astype(F32) * q_scale
            k = qkv[pl.ds(width + r, CH), :]
            v = qkv[pl.ds(2 * width + r, CH), :]
            q_hi = q.astype(BF)
            q_lo = (q - q_hi.astype(F32)).astype(BF)
            left = jnp.concatenate([k, k, bias], axis=0)
            right = jnp.concatenate([q_hi, q_lo, ones], axis=0)
            s = dg(left, right, 0, 0)
            if pending is not None:
                pending()
            m = jnp.max(s, axis=0, keepdims=True)
            e = jnp.exp2(s - m)
            reci = 1.0 / jnp.sum(e, axis=0, keepdims=True)
            e = e.astype(BF)
            expo[h] = e
            inv[h] = reci

            def pending(r=r, v=v, e=e, reci=reci):
                o32[pl.ds(r, CH), :] = jnp.dot(v, e, preferred_element_type=F32) * reci

        pending()

    def forward_sending(step, _):
        forward(step, 2, 21)
        return 0

    def forward_plain(step, _):
        forward(step, 0, 0)
        return 0

    lax.fori_loop(0, 6, forward_sending, 0)
    lax.fori_loop(6, HEADS // 2, forward_plain, 0)

    att[...] = o32[...].astype(BF)
    out_t = (x16[...].astype(F32) + dg(w_out[...], att[...], 0, 0)).astype(BF)
    wait_sent(send_a, 0)
    to_chunks(dg(seat[...], out_t, 1, 1), send_a)
    wait_got(got_c, 1)
    send_some(send_a, got_r, 2, 1, 4)
    send_own(send_a, got_r, 2)
    from_chunks(got_c)
    c16[...] = dg(rows[...], seat[...], 0, 0).astype(BF)
    d_att[...] = jnp.dot(w_out[...], c16[...], preferred_element_type=F32).astype(BF)
    grads[:width, :] = dg(att[...], c16[...], 1, 1).astype(BF)

    def backward(step, first_peer, sends):
        for i in range(sends):
            chunk_copy(send_a, got_r, 2, lax.rem(me + first_peer + step * sends + i, n)).start()
        row = iota((CH, PATCH), 0)
        pending = None
        for u in range(2):
            h = step * 2 + u
            r = pl.multiple_of(h * CH, CH)
            q = qkv[pl.ds(r, CH), :]
            k = qkv[pl.ds(width + r, CH), :]
            v = qkv[pl.ds(2 * width + r, CH), :]
            d_o = d_att[pl.ds(r, CH), :].astype(F32)
            reci = inv[h]
            delta = jnp.sum(d_o * o32[pl.ds(r, CH), :], axis=0, keepdims=True) * (-reci)
            d_o = d_o * reci
            d_hi = d_o.astype(BF)
            d_lo = (d_o - d_hi.astype(F32)).astype(BF)
            delta_hi = delta.astype(BF).astype(F32)
            delta_lo = delta - delta_hi
            extra = jnp.where(row == 0, delta_hi, jnp.where(row == 1, delta_lo, 0.0)).astype(BF)
            left = jnp.concatenate([v, v, pair], axis=0)
            right = jnp.concatenate([d_hi, d_lo, extra], axis=0)
            t = dg(left, right, 0, 0)
            d_v = dg(d_hi, expo[h], 1, 1)
            e = (expo[h].astype(F32) * t).astype(BF)
            if pending is not None:
                pending()
            expo[h] = e
            qkv[pl.ds(2 * width + r, CH), :] = d_v.astype(BF)

            def pending(r=r, k=k, q=q, h=h):
                e = expo[h]
                qkv[pl.ds(r, CH), :] = (jnp.dot(k, e, preferred_element_type=F32) * 0.25).astype(BF)
                qkv[pl.ds(width + r, CH), :] = (dg(q, e, 1, 1) * 0.25).astype(BF)

        pending()

    def backward_sending(step, _):
        backward(step, 4, 31)
        return 0

    early = EARLY * CH
    late = width - early
    depth = 4 * width // PLANE
    strip = depth // RING
    split = (width + 3 * early) // depth
    at_z = lax.rem(me // SIDE, RING)
    member = (me // (SIDE * RING)) * SIDE + lax.rem(me, SIDE)
    mine = lax.rem(member * MIX, PLANE)
    is_early = mine < split

    def in_plane(other_member):
        return (other_member // SIDE) * (SIDE * RING) + at_z * SIDE + lax.rem(other_member, SIDE)

    def block(ref, b):
        return ref.at[pl.ds(pl.multiple_of(b * depth, depth), depth), :]

    def strip_of(ref, z):
        return ref.at[pl.ds(pl.multiple_of(z * strip, strip), strip), :]

    def remote(src, dst, which, peer):
        return pltpu.make_async_remote_copy(
            src_ref=src, dst_ref=dst, send_sem=send_sem.at[which], recv_sem=recv_sem.at[which],
            device_id=(peer, rep), device_id_type=pl.DeviceIdType.MESH,
        )

    def send_blocks(lo, hi):
        def one(j, _):
            b = lo + lax.rem(j + member, hi - lo)
            peer = in_plane(lax.rem(b * MIX, PLANE))

            @pl.when(peer != me)
            def _():
                remote(block(grads, b), parts.at[member], 4, peer).start()

            @pl.when(peer == me)
            def _():
                pltpu.make_async_copy(block(grads, mine), parts.at[member], recv_sem.at[4]).start()

            return 0

        lax.fori_loop(0, hi - lo, one, 0)

    def along_z(j):
        z = lax.rem(at_z + j, RING)
        return z, (me // (SIDE * RING)) * (SIDE * RING) + z * SIDE + lax.rem(me, SIDE)

    def sum_block():
        wait_got(parts, 4)
        plane_sum[...] = jnp.sum(parts[...].astype(F32), axis=0)

        def one(j, _):
            z, peer = along_z(j)
            remote(strip_of(plane_sum, z), strips.at[at_z], 6, peer).start()
            return 0

        lax.fori_loop(1, RING, one, 0)
        pltpu.make_async_copy(strip_of(plane_sum, at_z), strips.at[at_z], recv_sem.at[6]).start()

    def swap():
        return pltpu.make_async_remote_copy(
            src_ref=total, dst_ref=other, send_sem=pair_sem.at[0], recv_sem=pair_sem.at[1],
            device_id=(me, 1 - rep), device_id_type=pl.DeviceIdType.MESH,
        )

    def swap_strip():
        wait_got(strips, 6)
        total[...] = jnp.sum(strips[...], axis=0)
        swap().start()

    def gather_strip():
        swap().wait()
        scaled[...] = (total[...] + other[...]) * factor

        def one(j, _):
            _, peer = along_z(j)
            remote(scaled, strip_of(done, at_z), 7, peer).start()
            return 0

        lax.fori_loop(1, RING, one, 0)
        pltpu.make_async_copy(scaled, strip_of(done, at_z), recv_sem.at[7]).start()

    def share_block():
        wait_got(done, 7)
        ready[...] = done[...].astype(BF)

        def one(j, _):
            remote(ready, block(whole, mine), 5, in_plane(lax.rem(member + j, PLANE))).start()
            return 0

        lax.fori_loop(1, PLANE, one, 0)
        pltpu.make_async_copy(ready, block(whole, mine), recv_sem.at[5]).start()

    def backward_late(step, _):
        backward(step, 0, 0)
        for after, job in enumerate((sum_block, swap_strip, gather_strip, share_block)):
            pl.when(is_early & (step == EARLY // 2 + after))(job)
        return 0

    lax.fori_loop(0, EARLY // 2, backward_sending, 0)
    at = width
    for p in range(3):
        grads[at : at + early, :] = dg(
            qkv[p * width : p * width + early, :], norm[...], 1, 1
        ).astype(BF)
        at += early
    send_blocks(0, split)
    lax.fori_loop(EARLY // 2, HEADS // 2, backward_late, 0)
    for p in range(3):
        grads[at : at + late, :] = dg(
            qkv[p * width + early : (p + 1) * width, :], norm[...], 1, 1
        ).astype(BF)
        at += late
    send_blocks(split, PLANE)

    d_norm = jnp.dot(w_qkv[...], qkv[...], preferred_element_type=F32)
    values = x16[...].astype(F32)
    center = jnp.mean(values, axis=0, keepdims=True)
    spread = jnp.mean(jnp.square(values - center), axis=0, keepdims=True)
    scale = lax.rsqrt(spread + 1e-05)
    unit = (values - center) * scale
    along = jnp.mean(d_norm * unit, axis=0, keepdims=True)
    level = jnp.mean(d_norm, axis=0, keepdims=True)
    d_rows = (c16[...].astype(F32) + scale * (d_norm - level - unit * along)).astype(BF)
    wait_sent(send_b, 1)
    to_chunks(dg(seat[...], d_rows, 1, 1), send_b)
    send_some(send_b, got_g, 3, 1, n)
    send_own(send_b, got_g, 3)

    is_late = jnp.logical_not(is_early)
    pl.when(is_late)(sum_block)
    wait_got(got_r, 2)
    from_chunks(got_r)
    pl.when(is_late)(swap_strip)
    out_r[...] = jnp.dot(back[...], rows[...], preferred_element_type=F32).astype(BF)
    pl.when(is_late)(gather_strip)
    pl.when(is_late)(share_block)
    wait_got(got_g, 3)
    from_chunks(got_g)
    out_g[...] = jnp.dot(back[...], rows[...], preferred_element_type=F32).astype(BF)
    pltpu.make_async_copy(whole, whole, recv_sem.at[5]).wait()
    pieces = []
    for p in range(3):
        at = width + p * early
        pieces.append(whole[at : at + early, :])
        at = width + 3 * early + p * late
        pieces.append(whole[at : at + late, :])
    out_wq[...] = jnp.transpose(jnp.concatenate(pieces, axis=0).astype(F32))
    out_wo[...] = whole[:width, :].astype(F32)
    wait_sent(send_a, 2)
    wait_sent(send_b, 3)
    for which, ref, copies in ((4, parts, PLANE - 1), (5, parts, PLANE - 1), (6, strips, RING - 1), (7, strips, RING - 1)):
        part = ref.at[pl.ds(0, copies)]
        pltpu.make_async_copy(part, part, send_sem.at[which]).wait()


def on_device(feats, cotangent, dest, pads, w_qkv, w_out):
    n = lax.axis_size("pts")
    points = feats.shape[1]
    width = feats.shape[2]
    depth = 4 * width // PLANE
    factor = float((n * lax.axis_size("rep") * points) ** (-0.5))
    vmem = pl.BlockSpec(memory_space=pltpu.VMEM)
    got = pl.pallas_call(
        functools.partial(kernel, n, factor),
        out_shape=(
            jax.ShapeDtypeStruct((points, width), BF),
            jax.ShapeDtypeStruct((points, width), BF),
            jax.ShapeDtypeStruct((width, 3 * width), F32),
            jax.ShapeDtypeStruct((width, width), F32),
        ),
        in_specs=[vmem, vmem, vmem, pl.BlockSpec(memory_space=pltpu.SMEM), vmem, vmem],
        out_specs=(vmem, vmem, vmem, vmem),
        scratch_shapes=[
            pltpu.VMEM((points, CAP * n), BF),
            pltpu.VMEM((CAP * n, PATCH), BF),
            pltpu.VMEM((n * CHUNK, 128), F32),
            *[pltpu.VMEM((n, CHUNK, 128), BF)] * 6,
            pltpu.VMEM((CAP * n, width), BF),
            pltpu.VMEM((width, PATCH), BF),
            pltpu.VMEM((width, PATCH), BF),
            pltpu.VMEM((width, PATCH), BF),
            pltpu.VMEM((3 * width, PATCH), BF),
            pltpu.VMEM((width, PATCH), BF),
            pltpu.VMEM((width, PATCH), BF),
            pltpu.VMEM((width, PATCH), F32),
            pltpu.VMEM((HEADS, 1, PATCH), F32),
            pltpu.VMEM((HEADS, PATCH, PATCH), BF),
            pltpu.VMEM((4 * width, width), BF),
            pltpu.VMEM((PLANE, depth, width), BF),
            pltpu.VMEM((depth, width), F32),
            pltpu.VMEM((RING, depth // RING, width), F32),
            pltpu.VMEM((depth // RING, width), F32),
            pltpu.VMEM((depth // RING, width), F32),
            pltpu.VMEM((depth // RING, width), F32),
            pltpu.VMEM((depth, width), F32),
            pltpu.VMEM((depth, width), BF),
            pltpu.VMEM((4 * width, width), BF),
            pltpu.SemaphoreType.DMA((8,)),
            pltpu.SemaphoreType.DMA((8,)),
            pltpu.SemaphoreType.DMA((2,)),
        ],
        compiler_params=pltpu.CompilerParams(
            collective_id=0, has_side_effects=True, vmem_limit_bytes=62 * 2**20
        ),
        cost_estimate=pl.CostEstimate(flops=4 * 10**9, bytes_accessed=4 * 10**6, transcendentals=17 * 10**6),
    )(feats[0], cotangent[0], dest, pads, w_qkv, w_out)
    return (got[0][None], got[1][None], got[2], got[3])


def solution(mesh):
    placed = (
        P("rep", "pts", None),
        P("rep", "pts", None),
        P("rep", "pts"),
        P("rep", "pts"),
        P(),
        P(),
    )
    return jax.shard_map(
        on_device,
        mesh=mesh,
        in_specs=placed,
        out_specs=(P("rep", "pts", None), P("rep", "pts", None), P(), P()),
        check_vma=False,
    )
```

```python
import functools

import jax
import jax.numpy as jnp
from jax import lax
from jax.experimental import pallas as pl
from jax.experimental.pallas import tpu as pltpu
from jax.sharding import PartitionSpec as P

HEADS = 16
CH = 16
PATCH = 1024
CAP = 10
CHUNK = 24
EARLY = 8
RING = 8
SIDE = 4
PLANE = SIDE * SIDE
MIX = 7
BF = jnp.bfloat16
F32 = jnp.float32


def dg(a, b, ca, cb):
    return lax.dot_general(a, b, (((ca,), (cb,)), ((), ())), preferred_element_type=F32)


def iota(shape, dim):
    return lax.broadcasted_iota(jnp.int32, shape, dim)


def kernel(
    n, factor,
    feats, cot, dest, pads, w_qkv, w_out,
    out_r, out_g, out_wq, out_wo,
    back, seat, stage, send_a, send_b, got_f, got_c, got_r, got_g,
    rows, x16, c16, norm, qkv, att, d_att, o32, inv, expo,
    grads, parts, plane_sum, strips, total, other, scaled, done, ready, whole,
    send_sem, recv_sem, pair_sem,
):
    me = lax.axis_index("pts")
    rep = lax.axis_index("rep")
    width = feats.shape[1]
    points = feats.shape[0]

    barrier = pltpu.get_barrier_semaphore()

    def greet(j, _):
        pl.semaphore_signal(
            barrier, inc=1, device_id=(lax.rem(me + j, n), rep), device_id_type=pl.DeviceIdType.MESH
        )
        return 0

    lax.fori_loop(1, n, greet, 0)
    pl.semaphore_signal(barrier, inc=1, device_id=(me, 1 - rep), device_id_type=pl.DeviceIdType.MESH)

    def chunk_copy(src, dst, which, peer):
        return pltpu.make_async_remote_copy(
            src_ref=src.at[peer],
            dst_ref=dst.at[me],
            send_sem=send_sem.at[which],
            recv_sem=recv_sem.at[which],
            device_id=(peer, rep),
            device_id_type=pl.DeviceIdType.MESH,
        )

    def send_some(src, dst, which, lo, hi):
        def one(j, _):
            chunk_copy(src, dst, which, lax.rem(me + j, n)).start()
            return 0

        lax.fori_loop(lo, hi, one, 0)

    def send_own(src, dst, which):
        pltpu.make_async_copy(src.at[me], dst.at[me], recv_sem.at[which]).start()

    def wait_got(dst, which):
        pltpu.make_async_copy(dst, dst, recv_sem.at[which]).wait()

    def wait_sent(src, which):
        part = src.at[pl.ds(0, n - 1)]
        pltpu.make_async_copy(part, part, send_sem.at[which]).wait()

    def to_chunks(values, dst):
        for k in range(CAP):
            for c in range(2):
                stage[pl.ds(c * CAP + k, n, stride=CHUNK), :] = values[
                    k * n : (k + 1) * n, c * 128 : (c + 1) * 128
                ]
        dst[...] = stage[...].reshape(n, CHUNK, 128).astype(BF)

    def from_chunks(src):
        stage[...] = src[...].astype(F32).reshape(n * CHUNK, 128)
        for k in range(CAP):
            for c in range(2):
                rows[k * n : (k + 1) * n, c * 128 : (c + 1) * 128] = stage[
                    pl.ds(c * CAP + k, n, stride=CHUNK), :
                ].astype(BF)

    target = dest[...]
    owner = lax.shift_right_logical(target, 10)
    code = (target & (PATCH - 1)) + 1
    owner_hot = (iota((n, points), 0) == owner).astype(F32).astype(BF)
    upper = (iota((points, points), 0) < iota((points, points), 1)).astype(F32).astype(BF)
    before = jnp.dot(owner_hot, upper, preferred_element_type=F32)
    rank = jnp.sum(before * owner_hot.astype(F32), axis=0, keepdims=True)
    place = rank * float(n) + owner.astype(F32)
    pick = (iota((CAP * n, points), 0) == place.astype(jnp.int32)).astype(F32).astype(BF)
    high = lax.shift_right_logical(code, 5).astype(F32)
    low = (code & 31).astype(F32)
    lane = iota((128, points), 0).astype(F32)
    marks = (jnp.where(lane == rank, high, 0.0) + jnp.where(lane == rank + 16.0, low, 0.0)).astype(BF)
    stage[...] = jnp.zeros(stage.shape, F32)
    stage[pl.ds(2 * CAP, n, stride=CHUNK), :] = dg(owner_hot, marks, 1, 1)
    to_chunks(jnp.dot(pick, feats[...], preferred_element_type=F32), send_a)
    to_chunks(jnp.dot(pick, cot[...], preferred_element_type=F32), send_b)

    pl.semaphore_wait(barrier, n)

    send_some(send_a, got_f, 0, 1, n)
    send_own(send_a, got_f, 0)
    place_col = jnp.transpose(jnp.broadcast_to(place, (8, points)))[:, :1].astype(jnp.int32)
    back[...] = (iota((points, CAP * n), 1) == place_col).astype(F32).astype(BF)
    wait_got(got_f, 0)
    send_some(send_b, got_c, 1, 1, 2)
    send_own(send_b, got_c, 1)

    from_chunks(got_f)
    marked = stage[pl.ds(2 * CAP, n, stride=CHUNK), :]
    for k in range(CAP):
        column = (32.0 * marked[:, k : k + 1] + marked[:, 16 + k : 17 + k]).astype(jnp.int32)
        seat[k * n : (k + 1) * n, :] = (iota((n, PATCH), 1) + 1 == column).astype(F32).astype(BF)
    x16[...] = dg(rows[...], seat[...], 0, 0).astype(BF)

    values = x16[...].astype(F32)
    center = jnp.mean(values, axis=0, keepdims=True)
    spread = jnp.mean(jnp.square(values - center), axis=0, keepdims=True)
    scale = lax.rsqrt(spread + 1e-05)
    norm[...] = ((values - center) * scale).astype(BF)
    qkv[...] = dg(w_qkv[...], norm[...], 0, 0).astype(BF)

    count = PATCH - pads[0, 0]
    first = iota((CH, PATCH), 0) == 0
    bias = jnp.where(first & (iota((CH, PATCH), 1) >= count), -1e30, 0.0).astype(BF)
    ones = jnp.where(iota((CH, PATCH), 0) == 0, 1.0, 0.0).astype(BF)
    pair = jnp.where(iota((CH, PATCH), 0) < 2, 1.0, 0.0).astype(BF)
    q_scale = float(CH ** -0.5 * 1.4426950408889634)

    def forward(step, first_peer, sends):
        for i in range(sends):
            chunk_copy(send_b, got_c, 1, lax.rem(me + first_peer + step * sends + i, n)).start()
        pending = None
        for u in range(2):
            h = step * 2 + u
            r = pl.multiple_of(h * CH, CH)
            q = qkv[pl.ds(r, CH), :].astype(F32) * q_scale
            k = qkv[pl.ds(width + r, CH), :]
            v = qkv[pl.ds(2 * width + r, CH), :]
            q_hi = q.astype(BF)
            q_lo = (q - q_hi.astype(F32)).astype(BF)
            left = jnp.concatenate([k, k, bias], axis=0)
            right = jnp.concatenate([q_hi, q_lo, ones], axis=0)
            s = dg(left, right, 0, 0)
            if pending is not None:
                pending()
            m = jnp.max(s, axis=0, keepdims=True)
            e = jnp.exp2(s - m)
            reci = 1.0 / jnp.sum(e, axis=0, keepdims=True)
            e = e.astype(BF)
            expo[h] = e
            inv[h] = reci

            def pending(r=r, v=v, e=e, reci=reci):
                o32[pl.ds(r, CH), :] = jnp.dot(v, e, preferred_element_type=F32) * reci

        pending()

    def forward_sending(step, _):
        forward(step, 2, 21)
        return 0

    def forward_plain(step, _):
        forward(step, 0, 0)
        return 0

    lax.fori_loop(0, 6, forward_sending, 0)
    lax.fori_loop(6, HEADS // 2, forward_plain, 0)

    att[...] = o32[...].astype(BF)
    out_t = (x16[...].astype(F32) + dg(w_out[...], att[...], 0, 0)).astype(BF)
    wait_sent(send_a, 0)
    to_chunks(dg(seat[...], out_t, 1, 1), send_a)
    wait_got(got_c, 1)
    send_some(send_a, got_r, 2, 1, 4)
    send_own(send_a, got_r, 2)
    from_chunks(got_c)
    c16[...] = dg(rows[...], seat[...], 0, 0).astype(BF)
    d_att[...] = jnp.dot(w_out[...], c16[...], preferred_element_type=F32).astype(BF)
    grads[:width, :] = dg(att[...], c16[...], 1, 1).astype(BF)

    def backward(step, first_peer, sends):
        for i in range(sends):
            chunk_copy(send_a, got_r, 2, lax.rem(me + first_peer + step * sends + i, n)).start()
        row = iota((CH, PATCH), 0)
        pending = None
        for u in range(2):
            h = step * 2 + u
            r = pl.multiple_of(h * CH, CH)
            q = qkv[pl.ds(r, CH), :]
            k = qkv[pl.ds(width + r, CH), :]
            v = qkv[pl.ds(2 * width + r, CH), :]
            d_o = d_att[pl.ds(r, CH), :].astype(F32)
            reci = inv[h]
            delta = jnp.sum(d_o * o32[pl.ds(r, CH), :], axis=0, keepdims=True) * (-reci)
            d_o = d_o * reci
            d_hi = d_o.astype(BF)
            d_lo = (d_o - d_hi.astype(F32)).astype(BF)
            delta_hi = delta.astype(BF).astype(F32)
            delta_lo = delta - delta_hi
            extra = jnp.where(row == 0, delta_hi, jnp.where(row == 1, delta_lo, 0.0)).astype(BF)
            left = jnp.concatenate([v, v, pair], axis=0)
            right = jnp.concatenate([d_hi, d_lo, extra], axis=0)
            t = dg(left, right, 0, 0)
            d_v = dg(d_hi, expo[h], 1, 1)
            e = (expo[h].astype(F32) * t).astype(BF)
            if pending is not None:
                pending()
            expo[h] = e
            qkv[pl.ds(2 * width + r, CH), :] = d_v.astype(BF)

            def pending(r=r, k=k, q=q, h=h):
                e = expo[h]
                qkv[pl.ds(r, CH), :] = (jnp.dot(k, e, preferred_element_type=F32) * 0.25).astype(BF)
                qkv[pl.ds(width + r, CH), :] = (dg(q, e, 1, 1) * 0.25).astype(BF)

        pending()

    def backward_sending(step, _):
        backward(step, 4, 31)
        return 0

    early = EARLY * CH
    late = width - early
    depth = 4 * width // PLANE
    strip = depth // RING
    split = (width + 3 * early) // depth
    at_z = lax.rem(me // SIDE, RING)
    member = (me // (SIDE * RING)) * SIDE + lax.rem(me, SIDE)
    mine = lax.rem(member * MIX, PLANE)
    is_early = mine < split

    def in_plane(other_member):
        return (other_member // SIDE) * (SIDE * RING) + at_z * SIDE + lax.rem(other_member, SIDE)

    def block(ref, b):
        return ref.at[pl.ds(pl.multiple_of(b * depth, depth), depth), :]

    def strip_of(ref, z):
        return ref.at[pl.ds(pl.multiple_of(z * strip, strip), strip), :]

    def remote(src, dst, which, peer):
        return pltpu.make_async_remote_copy(
            src_ref=src, dst_ref=dst, send_sem=send_sem.at[which], recv_sem=recv_sem.at[which],
            device_id=(peer, rep), device_id_type=pl.DeviceIdType.MESH,
        )

    def send_blocks(lo, hi):
        def one(j, _):
            b = lo + lax.rem(j + member, hi - lo)
            peer = in_plane(lax.rem(b * MIX, PLANE))

            @pl.when(peer != me)
            def _():
                remote(block(grads, b), parts.at[member], 4, peer).start()

            @pl.when(peer == me)
            def _():
                pltpu.make_async_copy(block(grads, mine), parts.at[member], recv_sem.at[4]).start()

            return 0

        lax.fori_loop(0, hi - lo, one, 0)

    def along_z(j):
        z = lax.rem(at_z + j, RING)
        return z, (me // (SIDE * RING)) * (SIDE * RING) + z * SIDE + lax.rem(me, SIDE)

    def sum_block():
        wait_got(parts, 4)
        plane_sum[...] = jnp.sum(parts[...].astype(F32), axis=0)

        def one(j, _):
            z, peer = along_z(j)
            remote(strip_of(plane_sum, z), strips.at[at_z], 6, peer).start()
            return 0

        lax.fori_loop(1, RING, one, 0)
        pltpu.make_async_copy(strip_of(plane_sum, at_z), strips.at[at_z], recv_sem.at[6]).start()

    def swap():
        return pltpu.make_async_remote_copy(
            src_ref=total, dst_ref=other, send_sem=pair_sem.at[0], recv_sem=pair_sem.at[1],
            device_id=(me, 1 - rep), device_id_type=pl.DeviceIdType.MESH,
        )

    def swap_strip():
        wait_got(strips, 6)
        total[...] = jnp.sum(strips[...], axis=0)
        swap().start()

    def gather_strip():
        swap().wait()
        scaled[...] = (total[...] + other[...]) * factor

        def one(j, _):
            _, peer = along_z(j)
            remote(scaled, strip_of(done, at_z), 7, peer).start()
            return 0

        lax.fori_loop(1, RING, one, 0)
        pltpu.make_async_copy(scaled, strip_of(done, at_z), recv_sem.at[7]).start()

    def share_block():
        wait_got(done, 7)
        ready[...] = done[...].astype(BF)

        def one(j, _):
            remote(ready, block(whole, mine), 5, in_plane(lax.rem(member + j, PLANE))).start()
            return 0

        lax.fori_loop(1, PLANE, one, 0)
        pltpu.make_async_copy(ready, block(whole, mine), recv_sem.at[5]).start()

    def backward_late(step, _):
        backward(step, 0, 0)
        for after, job in enumerate((sum_block, swap_strip, gather_strip)):
            pl.when(is_early & (step == EARLY // 2 + 1 + after))(job)
        return 0

    lax.fori_loop(0, EARLY // 2, backward_sending, 0)
    at = width
    for p in range(3):
        grads[at : at + early, :] = dg(
            qkv[p * width : p * width + early, :], norm[...], 1, 1
        ).astype(BF)
        at += early
    send_blocks(0, split)
    lax.fori_loop(EARLY // 2, HEADS // 2, backward_late, 0)
    for p in range(3):
        grads[at : at + late, :] = dg(
            qkv[p * width + early : (p + 1) * width, :], norm[...], 1, 1
        ).astype(BF)
        at += late
    send_blocks(split, PLANE)

    d_norm = jnp.dot(w_qkv[...], qkv[...], preferred_element_type=F32)
    values = x16[...].astype(F32)
    center = jnp.mean(values, axis=0, keepdims=True)
    spread = jnp.mean(jnp.square(values - center), axis=0, keepdims=True)
    scale = lax.rsqrt(spread + 1e-05)
    unit = (values - center) * scale
    along = jnp.mean(d_norm * unit, axis=0, keepdims=True)
    level = jnp.mean(d_norm, axis=0, keepdims=True)
    d_rows = (c16[...].astype(F32) + scale * (d_norm - level - unit * along)).astype(BF)
    wait_sent(send_b, 1)
    to_chunks(dg(seat[...], d_rows, 1, 1), send_b)
    send_some(send_b, got_g, 3, 1, n)
    send_own(send_b, got_g, 3)

    is_late = jnp.logical_not(is_early)
    pl.when(is_early)(share_block)
    pl.when(is_late)(sum_block)
    wait_got(got_r, 2)
    from_chunks(got_r)
    pl.when(is_late)(swap_strip)
    out_r[...] = jnp.dot(back[...], rows[...], preferred_element_type=F32).astype(BF)
    pl.when(is_late)(gather_strip)
    pl.when(is_late)(share_block)
    wait_got(got_g, 3)
    from_chunks(got_g)
    out_g[...] = jnp.dot(back[...], rows[...], preferred_element_type=F32).astype(BF)
    pltpu.make_async_copy(whole, whole, recv_sem.at[5]).wait()
    pieces = []
    for p in range(3):
        at = width + p * early
        pieces.append(whole[at : at + early, :])
        at = width + 3 * early + p * late
        pieces.append(whole[at : at + late, :])
    out_wq[...] = jnp.transpose(jnp.concatenate(pieces, axis=0).astype(F32))
    out_wo[...] = whole[:width, :].astype(F32)
    wait_sent(send_a, 2)
    wait_sent(send_b, 3)
    for which, ref, copies in ((4, parts, PLANE - 1), (5, parts, PLANE - 1), (6, strips, RING - 1), (7, strips, RING - 1)):
        part = ref.at[pl.ds(0, copies)]
        pltpu.make_async_copy(part, part, send_sem.at[which]).wait()


def on_device(feats, cotangent, dest, pads, w_qkv, w_out):
    n = lax.axis_size("pts")
    points = feats.shape[1]
    width = feats.shape[2]
    depth = 4 * width // PLANE
    factor = float((n * lax.axis_size("rep") * points) ** (-0.5))
    vmem = pl.BlockSpec(memory_space=pltpu.VMEM)
    got = pl.pallas_call(
        functools.partial(kernel, n, factor),
        out_shape=(
            jax.ShapeDtypeStruct((points, width), BF),
            jax.ShapeDtypeStruct((points, width), BF),
            jax.ShapeDtypeStruct((width, 3 * width), F32),
            jax.ShapeDtypeStruct((width, width), F32),
        ),
        in_specs=[vmem, vmem, vmem, pl.BlockSpec(memory_space=pltpu.SMEM), vmem, vmem],
        out_specs=(vmem, vmem, vmem, vmem),
        scratch_shapes=[
            pltpu.VMEM((points, CAP * n), BF),
            pltpu.VMEM((CAP * n, PATCH), BF),
            pltpu.VMEM((n * CHUNK, 128), F32),
            *[pltpu.VMEM((n, CHUNK, 128), BF)] * 6,
            pltpu.VMEM((CAP * n, width), BF),
            pltpu.VMEM((width, PATCH), BF),
            pltpu.VMEM((width, PATCH), BF),
            pltpu.VMEM((width, PATCH), BF),
            pltpu.VMEM((3 * width, PATCH), BF),
            pltpu.VMEM((width, PATCH), BF),
            pltpu.VMEM((width, PATCH), BF),
            pltpu.VMEM((width, PATCH), F32),
            pltpu.VMEM((HEADS, 1, PATCH), F32),
            pltpu.VMEM((HEADS, PATCH, PATCH), BF),
            pltpu.VMEM((4 * width, width), BF),
            pltpu.VMEM((PLANE, depth, width), BF),
            pltpu.VMEM((depth, width), F32),
            pltpu.VMEM((RING, depth // RING, width), F32),
            pltpu.VMEM((depth // RING, width), F32),
            pltpu.VMEM((depth // RING, width), F32),
            pltpu.VMEM((depth // RING, width), F32),
            pltpu.VMEM((depth, width), F32),
            pltpu.VMEM((depth, width), BF),
            pltpu.VMEM((4 * width, width), BF),
            pltpu.SemaphoreType.DMA((8,)),
            pltpu.SemaphoreType.DMA((8,)),
            pltpu.SemaphoreType.DMA((2,)),
        ],
        compiler_params=pltpu.CompilerParams(
            collective_id=0, has_side_effects=True, vmem_limit_bytes=62 * 2**20
        ),
        cost_estimate=pl.CostEstimate(flops=4 * 10**9, bytes_accessed=4 * 10**6, transcendentals=17 * 10**6),
    )(feats[0], cotangent[0], dest, pads, w_qkv, w_out)
    return (got[0][None], got[1][None], got[2], got[3])


def solution(mesh):
    placed = (
        P("rep", "pts", None),
        P("rep", "pts", None),
        P("rep", "pts"),
        P("rep", "pts"),
        P(),
        P(),
    )
    return jax.shard_map(
        on_device,
        mesh=mesh,
        in_specs=placed,
        out_specs=(P("rep", "pts", None), P("rep", "pts", None), P(), P()),
        check_vma=False,
    )
```
